256 devices in a mesh: ch: 128 (over x, z, y), src: 2 (over core).
Axes of the slice: x: 4, y: 4, z: 8, core: 2. Of those that a mesh axis runs over, the one named last changes fastest.
Arguments:
- spectra: float32 [8192, 2, 2048], P('ch'), may hold values from -6 to 6
- source_ids: int32 [256], replicated, may hold values from 0 to 8191
- offset_bins: int32 [8192, 256], P('ch', 'src'), may hold values from 0 to 959
- owner_slots: int32 [1024], replicated, may hold values from 0 to 1023, each once
Outputs:
- stacks: float32 [1024, 128], P(('ch', 'src'))
The draws below stay inside these ranges and needn't reach their ends.
All inputs are finite; a program needn't handle non-finite values.
Results may differ from the reference program's by a relative error of at most 0.0037.
Values sent between devices are 32-bit elements; how exact they have to be, the bound alone decides.
No kernel may reach another device: no remote copies, remote signals or barrier semaphores. Data moves between devices by JAX's collectives and lax.ppermute only.
A program may use at most 64 MiB of HBM per device.

```python
import math
import jax
import jax.numpy as jnp
import numpy as np
from jax import lax

NB = 2048
LAGS = 128
CHANNELS = 8192
NSRC = 256
NBINS = 1024


def place_ends(entries, own_key, smallest, largest):
    place = [jax.random.randint(jax.random.fold_in(own_key, axis), (), 0, length) for axis, length in enumerate(entries.shape)]
    main_axis = entries.shape.index(max(entries.shape))
    neighbour = place[:main_axis] + [(place[main_axis] + 1) % entries.shape[main_axis]] + place[main_axis + 1:]
    return entries.at[tuple(place)].set(smallest).at[tuple(neighbour)].set(largest)


def block_scale(rng, dims, split, low, high):
    factor_of, own = 1.0, jax.random.fold_in(rng, 6)
    for dim, blocks in split:
        draws = jnp.exp(jax.random.uniform(jax.random.fold_in(own, dim), (blocks,), jnp.float32, low / len(split), high / len(split)))
        factor_of = factor_of * jnp.repeat(draws, dims[dim] // blocks).reshape([-1 if axis == dim else 1 for axis in range(len(dims))])
    return factor_of


def rank_table(number_of, skew):
    weights = [(1 << 20) // math.isqrt(grade ** skew) + 1 for grade in range(1, number_of + 1)]
    deviation = 1 + sum(weights) // (1 << 30)
    return np.cumsum(np.array([max(1, weight // deviation) for weight in weights]))


def skewed_ids(stream_key, shape, count, lean):
    listing = rank_table(count, lean)
    pick = jax.random.randint(jax.random.fold_in(stream_key, 1), shape, 0, int(listing[count - 1]))
    grade = jnp.searchsorted(jnp.asarray(listing, jnp.int32), pick, side="right")
    return jax.random.permutation(jax.random.fold_in(stream_key, 2), count)[grade].astype(jnp.int32)


def scatter_about(rng, shape, spread, bound, cuts=(), kind=jnp.bfloat16):
    drawn = jax.random.normal(rng, shape, jnp.float32) * spread
    if len(cuts) > 0:
        drawn = block_scale(rng, shape, cuts, -0.22, 0.18) * drawn
    return jnp.clip(drawn, min=-bound, max=bound).astype(kind)


def setup_inputs(seed: int = 0) -> dict:
    arg_keys = jax.random.split(jax.random.key(seed), 5)
    spectra = scatter_about(arg_keys[0], (CHANNELS, 2, NB), 1.0, 6.0, ((0, 128),), jnp.float32)
    source_ids = place_ends(jax.random.randint(arg_keys[1], (NSRC,), 0, CHANNELS), jax.random.fold_in(arg_keys[1], 1), 0, CHANNELS - 1).astype(jnp.int32)
    offset_bins = place_ends(skewed_ids(arg_keys[2], (CHANNELS, NSRC), NBINS - NBINS // 16, 2), jax.random.fold_in(arg_keys[2], 3), 0, (NBINS - NBINS // 16) - 1).astype(jnp.int32)
    owner_slots = jax.random.permutation(arg_keys[3], NBINS).astype(jnp.int32)
    return dict(spectra=spectra, source_ids=source_ids, offset_bins=offset_bins, owner_slots=owner_slots)


receiver_block = 4

def lag_table(bins, lags):
    freq = lax.broadcasted_iota(jnp.int32, (bins, lags), 0)
    shift = lax.broadcasted_iota(jnp.int32, (bins, lags), 1) - lags // 2
    phase = freq * shift % bins
    angle = phase.astype(jnp.float32) * (2.0 * math.pi / bins)
    return jnp.concatenate([jnp.cos(angle), -jnp.sin(angle)], axis=0).astype(jnp.bfloat16)

def cross_rows(receivers, sources):
    rec_re = receivers[:, None, 0, :]
    rec_im = receivers[:, None, 1, :]
    src_re = sources[None, :, 0, :]
    src_im = sources[None, :, 1, :]
    real_part = rec_re * src_re + rec_im * src_im
    imag_part = rec_im * src_re - rec_re * src_im
    joined = jnp.concatenate([real_part, imag_part], axis=2)
    return joined.reshape(-1, joined.shape[2]).astype(jnp.bfloat16)

def reference(spectra, source_ids, offset_bins, owner_slots):
    sources = jnp.take(spectra, source_ids, axis=0)
    table = lag_table(NB, LAGS)
    scale = NB ** (-0.5)
    turns = CHANNELS // receiver_block

    def step(carry, turn):
        panel, counts = carry
        start = (turn * receiver_block).astype(jnp.int32)
        receivers = lax.dynamic_slice_in_dim(spectra, start, receiver_block, 0)
        rows = cross_rows(receivers, sources)
        corr = jnp.dot(rows, table, preferred_element_type=jnp.float32) * scale
        bins = lax.dynamic_slice_in_dim(offset_bins, start, receiver_block, 0).reshape(-1)
        panel = panel + jax.ops.segment_sum(corr, bins, num_segments=NBINS)
        counts = counts + jax.ops.segment_sum(jnp.ones(bins.shape, jnp.float32), bins, num_segments=NBINS)
        return ((panel, counts), None)
    start_carry = (jnp.zeros((NBINS, LAGS), jnp.float32), jnp.zeros((NBINS,), jnp.float32))
    (panel, counts), unused = lax.scan(step, start_carry, jnp.arange(turns, dtype=jnp.int32))
    stacked = panel / jnp.sqrt(jnp.maximum(counts, 1.0))[:, None]
    return jnp.zeros((NBINS, LAGS), jnp.float32).at[owner_slots].set(stacked)
```

```python
import jax
import jax.numpy as jnp
import numpy as np
from jax import lax
from jax.sharding import Mesh
from jax.sharding import PartitionSpec as P

LAGS = 128
CLASSES = 16
FFT = 256
HALF = FFT // 2 + 1
highest = lax.Precision.HIGHEST


def tables(bins):
    width = bins // CLASSES
    q = np.arange(width)
    f = np.arange(FFT)
    t = np.arange(width)
    spread = np.zeros((CLASSES, 2, width, HALF, 4))
    gain = np.zeros((CLASSES, HALF, 4))
    minus = (-f[:HALF]) % FFT
    for p in range(CLASSES):
        k = CLASSES * q + p
        d = np.exp(2j * np.pi * (np.outer(k, t) % bins) / bins) @ np.exp(-2j * np.pi * (np.outer(t, f) % FFT) / FFT)
        plus, back = d[:, :HALF], d[:, minus]
        spread[p, 0, :, :, 0], spread[p, 1, :, :, 0] = plus.real, -plus.imag
        spread[p, 0, :, :, 1], spread[p, 1, :, :, 1] = plus.imag, plus.real
        spread[p, 0, :, :, 2], spread[p, 1, :, :, 2] = back.real, -back.imag
        spread[p, 0, :, :, 3], spread[p, 1, :, :, 3] = -back.imag, -back.real
        odd = f[:HALF] % 2
        g = np.where(odd == 1, np.sin(np.pi * p / 16), np.cos(np.pi * p / 16))
        gain[p] = g[:, None]
        gain[p, :, 2:] *= np.where(odd == 1, -1.0, 1.0)[:, None]
    j = np.arange(LAGS)
    weight = np.where((f[:HALF] == 0) | (f[:HALF] == FFT // 2), 1.0, 2.0) / FFT
    angle = 2 * np.pi * (np.outer(f[:HALF], j) % FFT) / FFT
    c, s = np.cos(angle) * weight[:, None], np.sin(angle) * weight[:, None]
    odd = (f[:HALF] % 2 == 1)[:, None]
    back = np.stack([np.where(odd, s, c), np.where(odd, c, -s)], axis=1)
    back = back * (CLASSES * bins ** -1.5)
    sign = np.where(q % 2 == 1, -1.0, 1.0)
    return spread, gain, sign, back


def split(spectra):
    rows, two, bins = spectra.shape
    return spectra.reshape(rows, 2, bins // CLASSES, CLASSES).transpose(3, 0, 1, 2)


def per_device(spectra, source_ids, offset_bins, owner_slots):
    local, two, bins = spectra.shape
    count = offset_bins.shape[1]
    slots = owner_slots.shape[0]
    spread, gain, sign, back = tables(bins)
    width = bins // CLASSES
    src_rank = lax.axis_index("core")
    ch_axes = ("x", "z", "y")
    ch_rank = lax.axis_index(ch_axes)
    devices = 128
    flat = spectra.reshape(local, 2 * bins)
    chan_ids = ch_rank * local + lax.broadcasted_iota(jnp.int32, (1, local), 1)
    mine = lax.dynamic_slice_in_dim(source_ids, src_rank * count, count, 0)
    select = (mine[:, None] == chan_ids).astype(jnp.float32)
    picked = jnp.dot(select, flat, precision=highest, preferred_element_type=jnp.float32)
    parts = lax.all_to_all(picked.reshape(devices, count // devices, 2 * bins), ch_axes, 0, 0)
    home = jnp.sum(parts, axis=0)
    wide = jnp.broadcast_to(home[None], (devices,) + home.shape)
    sources = lax.all_to_all(wide, ch_axes, 0, 0).reshape(count, 2, bins)

    spread_c = jnp.asarray(spread.reshape(CLASSES, 2 * width, HALF * 4), jnp.float32)
    signed = split(spectra) * jnp.asarray(sign, jnp.float32)
    rec = jnp.einsum("pri,pif->prf", signed.reshape(CLASSES, local, 2 * width), spread_c, precision=lax.Precision.HIGH)
    rec = rec.reshape(CLASSES, local, HALF, 4) * jnp.asarray(gain, jnp.float32)[:, None]
    rec = rec.transpose(2, 1, 0, 3).reshape(HALF, local, CLASSES * 4)
    rec_high = rec.astype(jnp.bfloat16)
    rec_low = (rec - rec_high.astype(jnp.float32)).astype(jnp.bfloat16)
    rec = jnp.concatenate([rec_high, rec_low], axis=2)
    src = jnp.einsum("pri,pif->prf", split(sources).reshape(CLASSES, count, 2 * width), spread_c, precision=lax.Precision.HIGH)
    src = src.reshape(CLASSES, count, HALF, 4).astype(jnp.bfloat16)
    turned = jnp.stack([-src[..., 1], src[..., 0], -src[..., 3], src[..., 2]], axis=-1)
    src = src.transpose(2, 1, 0, 3).reshape(HALF, count, CLASSES * 4)
    turned = turned.transpose(2, 1, 0, 3).reshape(HALF, count, CLASSES * 4)
    both = jnp.stack([src, turned], axis=1).reshape(HALF, 2 * count, CLASSES * 4)
    both = jnp.concatenate([both, both], axis=2)
    prod = jnp.einsum("frk,fsk->frs", rec, both, preferred_element_type=jnp.float32).astype(jnp.bfloat16)
    prod = prod.reshape(HALF, local, 2, count)

    iota = lax.broadcasted_iota(jnp.int32, (slots, 1), 0)
    bin_of = jnp.sum(jnp.where(iota == owner_slots[None, :], lax.broadcasted_iota(jnp.int32, (1, slots), 1), 0), axis=1)
    member = bin_of[:, None, None] == offset_bins[None]
    counts = jnp.sum(member.astype(jnp.float32), axis=(1, 2))
    sums = lax.dot_general(
        member.astype(jnp.bfloat16), prod, (((1, 2), (1, 3)), ((), ())), preferred_element_type=jnp.float32
    )
    panel = jnp.dot(
        sums.reshape(slots, HALF * 2), jnp.asarray(back.reshape(HALF * 2, LAGS), jnp.float32), precision=highest
    )
    own = slots // (2 * devices)
    packed = jnp.concatenate(
        [panel.reshape(devices, 2, own * LAGS), jnp.pad(counts.reshape(devices, 2, own), ((0, 0), (0, 0), (0, LAGS - own)))],
        axis=2,
    )
    here = lax.dynamic_index_in_dim(packed, src_rank, 1, keepdims=False)
    there = lax.dynamic_index_in_dim(packed, 1 - src_rank, 1, keepdims=False)
    chip = here + lax.ppermute(there, "core", [(0, 1), (1, 0)])
    total = jnp.sum(lax.all_to_all(chip, ch_axes, 0, 0, tiled=True), axis=0)
    stack_sum = total[: own * LAGS].reshape(own, LAGS)
    stack_count = total[own * LAGS : own * LAGS + own]
    return stack_sum / jnp.sqrt(jnp.maximum(stack_count, 1.0))[:, None]


def solution(mesh):
    fine = Mesh(mesh.devices.reshape(4, 8, 4, 2), ("x", "z", "y", "core"))
    ch = ("x", "z", "y")
    placed = (P(ch, None, None), P(), P(ch, "core"), P())
    return jax.shard_map(
        per_device, mesh=fine, in_specs=placed, out_specs=P(ch + ("core",), None), check_vma=False
    )
```

```python
import functools

import jax
import jax.numpy as jnp
import numpy as np
from jax import lax
from jax.experimental import pallas as pl
from jax.experimental.pallas import tpu as pltpu
from jax.sharding import Mesh
from jax.sharding import PartitionSpec as P

LAGS = 128
CLASSES = 16
FFT = 256
WIDTH = 128
HALF = FFT // 2
PARTS = 4 * CLASSES
W_STEP = PARTS + 8
P_STEP = FFT + 8
X, Z, Y = 4, 8, 4
PLANE = ("x", "y")
CHIPS = ("x", "z", "y")
ROUNDS = 2
highest = lax.Precision.HIGHEST


def tables(bins):
    q = np.arange(WIDTH)
    f = np.arange(FFT)
    low = f[:HALF]
    minus = (-low) % FFT
    spread = np.zeros((CLASSES, 4, HALF, 2, WIDTH))
    gain = np.zeros((CLASSES, 4, HALF))
    for p in range(CLASSES):
        k = CLASSES * q + p
        d = np.exp(2j * np.pi * (np.outer(k, q) % bins) / bins) @ np.exp(-2j * np.pi * (np.outer(q, f) % FFT) / FFT)
        plus, back = d[:, :HALF].T.copy(), d[:, minus].T.conj().copy()
        spread[p, 0, :, 0], spread[p, 0, :, 1] = plus.real, -plus.imag
        spread[p, 1, :, 0], spread[p, 1, :, 1] = plus.imag, plus.real
        spread[p, 2, :, 0], spread[p, 2, :, 1] = back.real, back.imag
        spread[p, 3, :, 0], spread[p, 3, :, 1] = back.imag, -back.real
        last = d[:, HALF]
        spread[p, 2, 0, 0], spread[p, 2, 0, 1] = last.real, -last.imag
        spread[p, 3, 0, 0], spread[p, 3, 0, 1] = last.imag, last.real
        odd = low % 2 == 1
        gain[p] = np.where(odd, np.sin(np.pi * p / 16), np.cos(np.pi * p / 16))
        gain[p, 2:] *= np.where(odd, -1.0, 1.0)
    j = np.arange(LAGS)
    angle = 2 * np.pi * (np.outer(low, j) % FFT) / FFT
    c, s = 2 * np.cos(angle) / FFT, 2 * np.sin(angle) / FFT
    odd = (low % 2 == 1)[:, None]
    back = np.stack([np.where(odd, s, c), np.where(odd, c, -s)])
    back[0, 0] = 2 / FFT
    back[1, 0] = 2 * np.where(j % 2 == 1, -1.0, 1.0) / FFT
    back = back.reshape(FFT, LAGS) * (CLASSES * bins ** -1.5)
    gain = gain.transpose(2, 1, 0)
    weights = np.stack([gain, gain * np.array([1.0, -1.0, 1.0, -1.0])[:, None]])
    weights[0, 0, 2:] = 0
    weights[1, 0, :2], weights[1, 0, 2:] = 0, gain[0, 2:]
    weights = np.pad(weights.reshape(2, HALF, PARTS), ((0, 0), (0, 0), (0, 128 - PARTS)))
    return spread.reshape(CLASSES, 4 * HALF, 2 * WIDTH), weights, back


def high_low(values):
    high = np.asarray(values, np.float32).astype(jnp.bfloat16)
    low = (np.asarray(values, np.float32) - high.astype(np.float32)).astype(jnp.bfloat16)
    return jnp.asarray(high), jnp.asarray(low)


def by_class(rows):
    count, two, bins = rows.shape
    return rows.reshape(count, 2, WIDTH, CLASSES).transpose(0, 3, 1, 2)


def nt(a, b):
    return lax.dot_general(a, b, (((1,), (1,)), ((), ())), preferred_element_type=jnp.float32)


def split_here(values):
    high = values.astype(jnp.bfloat16)
    return high, (values - high.astype(jnp.float32)).astype(jnp.bfloat16)


def stack_kernel(z_ref, th_ref, tl_ref, a_ref, bins_ref, slot_ref, bh_ref, bl_ref, out_ref, w_ref, p_ref, acc_ref):
    local = bins_ref.shape[0]

    for p in range(CLASSES):
        zh, zl = split_here(z_ref[:, p * 2 * WIDTH : (p + 1) * 2 * WIDTH])
        u = nt(th_ref[p], zh) + nt(tl_ref[p], zh) + nt(th_ref[p], zl)
        for c in range(4):
            w_ref[pl.ds(c * CLASSES + p, HALF, stride=W_STEP), :] = u[c * HALF : (c + 1) * HALF]

    @pl.loop(0, HALF, unroll=16)
    def _(f):
        w = w_ref[pl.ds(pl.multiple_of(f * W_STEP, 8), PARTS), :].astype(jnp.bfloat16)
        o = jnp.dot(a_ref[f], jnp.concatenate([w, w], axis=0), preferred_element_type=jnp.float32)
        p_ref[pl.ds(f, local, stride=P_STEP), :] = o[:local]
        p_ref[pl.ds(f + HALF, local, stride=P_STEP), :] = o[local:]

    acc_ref[...] = jnp.zeros_like(acc_ref)
    group = 8

    @pl.loop(0, local // group)
    def _(g):
        member, prod = [], []
        for i in range(group):
            r = g * group + i
            mine = slot_ref[...] == bins_ref[pl.ds(r, 1), :]
            member.append(jnp.where(mine, 1.0, 0.0).astype(jnp.bfloat16))
            prod.append(p_ref[pl.ds(pl.multiple_of(r * P_STEP, 8), FFT), :].astype(jnp.bfloat16))
        acc_ref[...] += nt(jnp.concatenate(member, axis=1), jnp.concatenate(prod, axis=1))

    ah, al = split_here(acc_ref[...])
    out_ref[...] = (
        jnp.dot(ah, bh_ref[...], preferred_element_type=jnp.float32)
        + jnp.dot(al, bh_ref[...], preferred_element_type=jnp.float32)
        + jnp.dot(ah, bl_ref[...], preferred_element_type=jnp.float32)
    )


def stacked(sources, spread_h, spread_l, receivers, bins, bin_of, back_h, back_l):
    local = bins.shape[0]
    slots = bin_of.shape[0]
    vmem = pl.BlockSpec(memory_space=pltpu.VMEM)
    return pl.pallas_call(
        stack_kernel,
        out_shape=jax.ShapeDtypeStruct((slots, LAGS), jnp.float32),
        in_specs=[vmem] * 8,
        out_specs=vmem,
        scratch_shapes=[
            pltpu.VMEM((HALF * W_STEP, 128), jnp.float32),
            pltpu.VMEM((local * P_STEP, 128), jnp.float32),
            pltpu.VMEM((slots, FFT), jnp.float32),
        ],
        compiler_params=pltpu.CompilerParams(vmem_limit_bytes=48 * 1024 * 1024),
        cost_estimate=pl.CostEstimate(flops=9 * 10**9, bytes_accessed=16 * 2**20, transcendentals=0),
    )(sources, spread_h, spread_l, receivers, bins, bin_of, back_h, back_l)


def receiver_kernel(z_ref, th_ref, tl_ref, gain_ref, out_ref, t_ref, v_ref):
    local = z_ref.shape[0]
    block = 2 * WIDTH

    @pl.loop(0, t_ref.shape[0] // block)
    def _(i):
        at = pl.multiple_of(i * block, block)
        t_ref[pl.ds(at, block), :local] = z_ref[:, pl.ds(at, block)].T

    odd = lax.broadcasted_iota(jnp.int32, (2 * WIDTH, local), 0) % 2 == 1
    bins = t_ref.shape[0] // 2
    for p in range(CLASSES):
        z = jnp.concatenate([t_ref[pl.ds(i * bins + p, WIDTH, stride=CLASSES), :][:, :local] for i in range(2)], axis=0)
        zh, zl = split_here(jnp.where(odd, -z, z))
        u = (
            jnp.dot(th_ref[p], zh, preferred_element_type=jnp.float32)
            + jnp.dot(tl_ref[p], zh, preferred_element_type=jnp.float32)
            + jnp.dot(th_ref[p], zl, preferred_element_type=jnp.float32)
        )
        for c in range(4):
            v_ref[pl.ds(c * CLASSES + p, HALF, stride=W_STEP), :local] = u[c * HALF : (c + 1) * HALF]

    def place(f, swap):
        v = v_ref[pl.ds(pl.multiple_of(f * W_STEP, 8), PARTS), :local]
        a, b, c, d = (v[i * CLASSES : (i + 1) * CLASSES] for i in range(4))
        w = jnp.concatenate([b, a, d, c], axis=0) if swap else v
        real = v.T * gain_ref[0, pl.ds(f, 1), :PARTS]
        imag = w.T * gain_ref[1, pl.ds(f, 1), :PARTS]
        high, low = split_here(jnp.concatenate([real, imag], axis=0))
        out_ref[f] = jnp.concatenate([high, low], axis=1)

    @pl.loop(0, HALF, unroll=8)
    def _(f):
        place(f, True)

    place(0, False)


def receiver_side(flat, spread_h, spread_l, gain):
    local, width = flat.shape
    vmem = pl.BlockSpec(memory_space=pltpu.VMEM)
    return pl.pallas_call(
        receiver_kernel,
        out_shape=jax.ShapeDtypeStruct((HALF, 2 * local, 2 * PARTS), jnp.bfloat16),
        in_specs=[vmem] * 4,
        out_specs=vmem,
        scratch_shapes=[pltpu.VMEM((width, 128), jnp.float32), pltpu.VMEM((HALF * W_STEP, 128), jnp.float32)],
        compiler_params=pltpu.CompilerParams(vmem_limit_bytes=40 * 1024 * 1024),
        cost_estimate=pl.CostEstimate(flops=6 * 10**9, bytes_accessed=14 * 2**20, transcendentals=0),
    )(flat, spread_h, spread_l, gain)


def where_of(ids, local):
    chip = ids // local
    return chip, (chip // Y) % Z, (chip // (Z * Y)) * Y + chip % Y


def fits(ids, local):
    chip, plane, _ = where_of(ids, local)
    per_chip = jnp.sum((chip[:, None] == chip[None, :]).astype(jnp.int32), axis=1)
    per_plane = jnp.sum((plane[:, None] == plane[None, :]).astype(jnp.int32), axis=1)
    return (jnp.max(per_chip) <= X * Y) & (jnp.max(per_plane) <= ROUNDS * X * Y)


def select_rows(table, rows):
    return jnp.dot(table.astype(jnp.float32), rows, precision=highest, preferred_element_type=jnp.float32)


def bin_counts(bins, slots, owner_slots):
    flat = bins.reshape(1, -1)
    digit = lax.broadcasted_iota(jnp.int32, (32, 1), 0)
    high = (flat // 32 == digit).astype(jnp.bfloat16)
    low = (flat % 32 == digit).astype(jnp.bfloat16)
    per_bin = nt(high, low).reshape(1, slots)
    at = lax.broadcasted_iota(jnp.int32, (slots, 1), 0) == owner_slots[None, :]
    return jnp.sum(jnp.where(at, per_bin, 0.0), axis=1)


def per_device(spectra, source_ids, offset_bins, owner_slots):
    local, two, bins = spectra.shape
    count = offset_bins.shape[1]
    slots = owner_slots.shape[0]
    spots = X * Y
    rows = count // spots
    spread, gain, back = tables(bins)
    spread_h, spread_l = high_low(spread)
    back_h, back_l = high_low(back)
    src_rank = lax.axis_index("core")
    ch_rank = lax.axis_index(CHIPS)
    my_plane = lax.axis_index("z")
    my_spot = lax.axis_index(PLANE)
    mine = lax.dynamic_slice_in_dim(source_ids, src_rank * count, count, 0)
    chip, plane, spot = where_of(mine, local)
    key = (plane * spots + spot) * count + lax.iota(jnp.int32, count)
    rank = jnp.sum((key[None, :] < key[:, None]).astype(jnp.int32), axis=1)
    dest = rank % spots
    flat = spectra.reshape(local, 2 * bins)

    row = lax.broadcasted_iota(jnp.int32, (spots, 1), 0)
    owned = jnp.where(chip == ch_rank, mine % local, -1)
    channel = jnp.max(jnp.where(dest[None, :] == row, owned[None, :], -1), axis=1)
    picked = select_rows(channel[:, None] == lax.broadcasted_iota(jnp.int32, (1, local), 1), flat)
    picked = by_class(picked.reshape(spots, 2, bins)).reshape(spots, 2 * bins)
    came = lax.all_to_all(picked, PLANE, 0, 0, tiled=True)

    before = jnp.sum((plane[None, :] < lax.broadcasted_iota(jnp.int32, (Z, 1), 0)).astype(jnp.int32), axis=1)
    first = before + (my_spot - before) % spots
    turn = (rank - first[plane]) // spots
    here = (plane == my_plane) & (dest == my_spot)
    at = here[None, :] & (turn[None, :] == lax.broadcasted_iota(jnp.int32, (ROUNDS, 1), 0))
    sender = jnp.max(jnp.where(at, spot[None, :], -1), axis=1)
    kept = select_rows(sender[:, None] == lax.broadcasted_iota(jnp.int32, (1, spots), 1), came)
    wide = jnp.broadcast_to(kept[None], (Z,) + kept.shape)
    came = lax.all_to_all(wide, "z", 0, 0, tiled=True).reshape(Z * ROUNDS, 2 * bins)

    at = rank[None, :] == lax.broadcasted_iota(jnp.int32, (rows, 1), 0) * spots + my_spot
    sender = jnp.max(jnp.where(at, (plane * ROUNDS + turn)[None, :], -1), axis=1)
    kept = select_rows(sender[:, None] == lax.broadcasted_iota(jnp.int32, (1, Z * ROUNDS), 1), came)
    kept, later = lax.optimization_barrier((kept, flat))
    wide = jnp.broadcast_to(kept[None], (spots,) + kept.shape)
    routed = lax.all_to_all(wide, PLANE, 0, 0, tiled=True).reshape(count, 2 * bins)
    receivers = receiver_side(later, spread_h, spread_l, jnp.asarray(gain, jnp.float32))

    place = dest * rows + rank // spots
    placing = place[:, None] == lax.broadcasted_iota(jnp.int32, (count, count), 1)

    def summed():
        ids = jnp.sum(jnp.where(placing, mine[:, None], 0), axis=0)
        chan_ids = ch_rank * local + lax.broadcasted_iota(jnp.int32, (1, local), 1)
        found = select_rows(ids[:, None] == chan_ids, flat)
        home = jnp.sum(lax.all_to_all(found, CHIPS, 0, 0, tiled=True), axis=0, keepdims=True)
        home = by_class(home.reshape(1, 2, bins)).reshape(1, 2 * bins)
        return lax.all_to_all(jnp.broadcast_to(home, (count, 2 * bins)), CHIPS, 0, 0, tiled=True)

    ok = fits(source_ids[:count], local) & fits(source_ids[count:], local)
    sources = lax.cond(ok, lambda: routed, summed)

    iota = lax.broadcasted_iota(jnp.int32, (slots, 1), 0)
    bin_of = jnp.sum(jnp.where(iota == owner_slots[None, :], lax.broadcasted_iota(jnp.int32, (1, slots), 1), 0), axis=1)
    bins_here = select_rows(offset_bins, placing.astype(jnp.float32)).astype(jnp.int32)
    counts = bin_counts(offset_bins, slots, owner_slots)
    bin_wide = jnp.broadcast_to(bin_of[:, None], (slots, 128))
    panel = stacked(sources, spread_h, spread_l, receivers, bins_here, bin_wide, back_h, back_l)

    devices = X * Y * Z
    own = slots // (2 * devices)
    packed = jnp.concatenate(
        [panel.reshape(devices, 2, own * LAGS), jnp.pad(counts.reshape(devices, 2, own), ((0, 0), (0, 0), (0, LAGS - own)))],
        axis=2,
    )
    here = lax.dynamic_index_in_dim(packed, src_rank, 1, keepdims=False)
    there = lax.dynamic_index_in_dim(packed, 1 - src_rank, 1, keepdims=False)
    halves = here + lax.ppermute(there, "core", [(0, 1), (1, 0)])
    total = jnp.sum(lax.all_to_all(halves, CHIPS, 0, 0, tiled=True), axis=0)
    stack_sum = total[: own * LAGS].reshape(own, LAGS)
    stack_count = total[own * LAGS : own * LAGS + own]
    return stack_sum / jnp.sqrt(jnp.maximum(stack_count, 1.0))[:, None]


def solution(mesh):
    fine = Mesh(mesh.devices.reshape(X, Z, Y, 2), ("x", "z", "y", "core"))
    placed = (P(CHIPS, None, None), P(), P(CHIPS, "core"), P())
    return jax.shard_map(
        per_device, mesh=fine, in_specs=placed, out_specs=P(CHIPS + ("core",), None), check_vma=False
    )
```

```python
import functools

import jax
import jax.numpy as jnp
import numpy as np
from jax import lax
from jax.experimental import pallas as pl
from jax.experimental.pallas import tpu as pltpu
from jax.sharding import Mesh
from jax.sharding import PartitionSpec as P

LAGS = 128
CLASSES = 16
FFT = 256
WIDTH = 128
HALF = FFT // 2
PARTS = 4 * CLASSES
W_STEP = PARTS + 8
P_STEP = FFT + 8
X, Z, Y = 4, 8, 4
PLANE = ("x", "y")
CHIPS = ("x", "z", "y")
ROUNDS = 2
GROUPS = 2
highest = lax.Precision.HIGHEST


def tables(bins):
    q = np.arange(WIDTH)
    f = np.arange(FFT)
    low = f[:HALF]
    minus = (-low) % FFT
    spread = np.zeros((CLASSES, 4, HALF, 2, WIDTH))
    gain = np.zeros((CLASSES, 4, HALF))
    for p in range(CLASSES):
        k = CLASSES * q + p
        d = np.exp(2j * np.pi * (np.outer(k, q) % bins) / bins) @ np.exp(-2j * np.pi * (np.outer(q, f) % FFT) / FFT)
        plus, back = d[:, :HALF].T.copy(), d[:, minus].T.conj().copy()
        spread[p, 0, :, 0], spread[p, 0, :, 1] = plus.real, -plus.imag
        spread[p, 1, :, 0], spread[p, 1, :, 1] = plus.imag, plus.real
        spread[p, 2, :, 0], spread[p, 2, :, 1] = back.real, back.imag
        spread[p, 3, :, 0], spread[p, 3, :, 1] = back.imag, -back.real
        last = d[:, HALF]
        spread[p, 2, 0, 0], spread[p, 2, 0, 1] = last.real, -last.imag
        spread[p, 3, 0, 0], spread[p, 3, 0, 1] = last.imag, last.real
        odd = low % 2 == 1
        gain[p] = np.where(odd, np.sin(np.pi * p / 16), np.cos(np.pi * p / 16))
        gain[p, 2:] *= np.where(odd, -1.0, 1.0)
    j = np.arange(LAGS)
    angle = 2 * np.pi * (np.outer(low, j) % FFT) / FFT
    c, s = 2 * np.cos(angle) / FFT, 2 * np.sin(angle) / FFT
    odd = (low % 2 == 1)[:, None]
    back = np.stack([np.where(odd, s, c), np.where(odd, c, -s)])
    back[0, 0] = 2 / FFT
    back[1, 0] = 2 * np.where(j % 2 == 1, -1.0, 1.0) / FFT
    back = back.reshape(FFT, LAGS) * (CLASSES * bins ** -1.5)
    gain = gain.transpose(2, 1, 0)
    weights = np.stack([gain, gain * np.array([1.0, -1.0, 1.0, -1.0])[:, None]])
    weights[0, 0, 2:] = 0
    weights[1, 0, :2], weights[1, 0, 2:] = 0, gain[0, 2:]
    weights = np.pad(weights.reshape(2, HALF, PARTS), ((0, 0), (0, 0), (0, 128 - PARTS)))
    return spread.reshape(CLASSES, 4 * HALF, 2 * WIDTH), weights, back


def high_low(values):
    high = np.asarray(values, np.float32).astype(jnp.bfloat16)
    low = (np.asarray(values, np.float32) - high.astype(np.float32)).astype(jnp.bfloat16)
    return jnp.asarray(high), jnp.asarray(low)


def by_class(rows):
    count, two, bins = rows.shape
    return rows.reshape(count, 2, WIDTH, CLASSES).transpose(0, 3, 1, 2)


def nt(a, b):
    return lax.dot_general(a, b, (((1,), (1,)), ((), ())), preferred_element_type=jnp.float32)


def split_here(values):
    high = values.astype(jnp.bfloat16)
    return high, (values - high.astype(jnp.float32)).astype(jnp.bfloat16)


def stack_kernel(
    sources, high, low, receivers, bins_ref, slot_ref, bh_ref, bl_ref,
    out_ref, w_ref, p_ref, acc_ref, z_ref, th_ref, tl_ref, a_ref, sems,
):
    local = bins_ref.shape[0]
    group = CLASSES // GROUPS
    whole = [(sources, z_ref)]
    for g in range(GROUPS):
        part = pl.ds(g * group, group)
        whole += [(high.at[part], th_ref.at[part]), (low.at[part], tl_ref.at[part])]
    whole += [(receivers, a_ref)]
    copies = [pltpu.make_async_copy(a, b, sems.at[i]) for i, (a, b) in enumerate(whole)]
    for copy in copies:
        copy.start()
    copies[0].wait()

    for p in range(CLASSES):
        if p % group == 0:
            copies[1 + 2 * (p // group)].wait()
            copies[2 + 2 * (p // group)].wait()
        zh, zl = split_here(z_ref[:, p * 2 * WIDTH : (p + 1) * 2 * WIDTH])
        u = nt(th_ref[p], zh) + nt(tl_ref[p], zh) + nt(th_ref[p], zl)
        for c in range(4):
            w_ref[pl.ds(c * CLASSES + p, HALF, stride=W_STEP), :] = u[c * HALF : (c + 1) * HALF]

    copies[-1].wait()

    @pl.loop(0, HALF, unroll=16)
    def _(f):
        w = w_ref[pl.ds(pl.multiple_of(f * W_STEP, 8), PARTS), :].astype(jnp.bfloat16)
        o = jnp.dot(a_ref[f], jnp.concatenate([w, w], axis=0), preferred_element_type=jnp.float32)
        p_ref[pl.ds(f, local, stride=P_STEP), :] = o[:local]
        p_ref[pl.ds(f + HALF, local, stride=P_STEP), :] = o[local:]

    acc_ref[...] = jnp.zeros_like(acc_ref)
    some = 8

    @pl.loop(0, local // some)
    def _(g):
        member, prod = [], []
        for i in range(some):
            r = g * some + i
            mine = slot_ref[...] == bins_ref[pl.ds(r, 1), :]
            member.append(jnp.where(mine, 1.0, 0.0).astype(jnp.bfloat16))
            prod.append(p_ref[pl.ds(pl.multiple_of(r * P_STEP, 8), FFT), :].astype(jnp.bfloat16))
        acc_ref[...] += nt(jnp.concatenate(member, axis=1), jnp.concatenate(prod, axis=1))

    ah, al = split_here(acc_ref[...])
    out_ref[...] = (
        jnp.dot(ah, bh_ref[...], preferred_element_type=jnp.float32)
        + jnp.dot(al, bh_ref[...], preferred_element_type=jnp.float32)
        + jnp.dot(ah, bl_ref[...], preferred_element_type=jnp.float32)
    )


def stacked(sources, spread_h, spread_l, receivers, bins, bin_of, back_h, back_l):
    local = bins.shape[0]
    slots = bin_of.shape[0]
    vmem = pl.BlockSpec(memory_space=pltpu.VMEM)
    return pl.pallas_call(
        stack_kernel,
        out_shape=jax.ShapeDtypeStruct((slots, LAGS), jnp.float32),
        in_specs=[pl.BlockSpec(memory_space=pl.ANY)] * 4 + [vmem] * 4,
        out_specs=vmem,
        scratch_shapes=[
            pltpu.VMEM((HALF * W_STEP, 128), jnp.float32),
            pltpu.VMEM((local * P_STEP, 128), jnp.float32),
            pltpu.VMEM((slots, FFT), jnp.float32),
            pltpu.VMEM(sources.shape, jnp.float32),
            pltpu.VMEM(spread_h.shape, jnp.bfloat16),
            pltpu.VMEM(spread_h.shape, jnp.bfloat16),
            pltpu.VMEM(receivers.shape, jnp.bfloat16),
            pltpu.SemaphoreType.DMA((2 * GROUPS + 2,)),
        ],
        compiler_params=pltpu.CompilerParams(vmem_limit_bytes=50 * 1024 * 1024),
        cost_estimate=pl.CostEstimate(flops=9 * 10**9, bytes_accessed=16 * 2**20, transcendentals=0),
    )(sources, spread_h, spread_l, receivers, bins, bin_of, back_h, back_l)


def receiver_kernel(z_ref, th_ref, tl_ref, gain_ref, out_ref, t_ref, v_ref):
    local = z_ref.shape[0]
    block = 2 * WIDTH

    @pl.loop(0, t_ref.shape[0] // block)
    def _(i):
        at = pl.multiple_of(i * block, block)
        t_ref[pl.ds(at, block), :local] = z_ref[:, pl.ds(at, block)].T

    odd = lax.broadcasted_iota(jnp.int32, (2 * WIDTH, local), 0) % 2 == 1
    bins = t_ref.shape[0] // 2
    for p in range(CLASSES):
        z = jnp.concatenate([t_ref[pl.ds(i * bins + p, WIDTH, stride=CLASSES), :][:, :local] for i in range(2)], axis=0)
        zh, zl = split_here(jnp.where(odd, -z, z))
        u = (
            jnp.dot(th_ref[p], zh, preferred_element_type=jnp.float32)
            + jnp.dot(tl_ref[p], zh, preferred_element_type=jnp.float32)
            + jnp.dot(th_ref[p], zl, preferred_element_type=jnp.float32)
        )
        for c in range(4):
            v_ref[pl.ds(c * CLASSES + p, HALF, stride=W_STEP), :local] = u[c * HALF : (c + 1) * HALF]

    def place(f, swap):
        v = v_ref[pl.ds(pl.multiple_of(f * W_STEP, 8), PARTS), :local]
        a, b, c, d = (v[i * CLASSES : (i + 1) * CLASSES] for i in range(4))
        w = jnp.concatenate([b, a, d, c], axis=0) if swap else v
        real = v.T * gain_ref[0, pl.ds(f, 1), :PARTS]
        imag = w.T * gain_ref[1, pl.ds(f, 1), :PARTS]
        high, low = split_here(jnp.concatenate([real, imag], axis=0))
        out_ref[f] = jnp.concatenate([high, low], axis=1)

    @pl.loop(0, HALF, unroll=8)
    def _(f):
        place(f, True)

    place(0, False)


def receiver_side(flat, spread_h, spread_l, gain):
    local, width = flat.shape
    vmem = pl.BlockSpec(memory_space=pltpu.VMEM)
    return pl.pallas_call(
        receiver_kernel,
        out_shape=jax.ShapeDtypeStruct((HALF, 2 * local, 2 * PARTS), jnp.bfloat16),
        in_specs=[vmem] * 4,
        out_specs=vmem,
        scratch_shapes=[pltpu.VMEM((width, 128), jnp.float32), pltpu.VMEM((HALF * W_STEP, 128), jnp.float32)],
        compiler_params=pltpu.CompilerParams(vmem_limit_bytes=26 * 1024 * 1024),
        cost_estimate=pl.CostEstimate(flops=6 * 10**9, bytes_accessed=14 * 2**20, transcendentals=0),
    )(flat, spread_h, spread_l, gain)


def where_of(ids, local):
    chip = ids // local
    return chip, (chip // Y) % Z, (chip // (Z * Y)) * Y + chip % Y


def fits(ids, local):
    chip, plane, _ = where_of(ids, local)
    per_chip = jnp.sum((chip[:, None] == chip[None, :]).astype(jnp.int32), axis=1)
    per_plane = jnp.sum((plane[:, None] == plane[None, :]).astype(jnp.int32), axis=1)
    return (jnp.max(per_chip) <= X * Y) & (jnp.max(per_plane) <= ROUNDS * X * Y)


def select_rows(table, rows):
    return jnp.dot(table.astype(jnp.float32), rows, precision=highest, preferred_element_type=jnp.float32)


def bin_counts(bins, slots, owner_slots):
    flat = bins.reshape(1, -1)
    digit = lax.broadcasted_iota(jnp.int32, (32, 1), 0)
    high = (flat // 32 == digit).astype(jnp.bfloat16)
    low = (flat % 32 == digit).astype(jnp.bfloat16)
    per_bin = nt(high, low).reshape(1, slots)
    at = lax.broadcasted_iota(jnp.int32, (slots, 1), 0) == owner_slots[None, :]
    return jnp.sum(jnp.where(at, per_bin, 0.0), axis=1)


def per_device(spectra, source_ids, offset_bins, owner_slots):
    local, two, bins = spectra.shape
    count = offset_bins.shape[1]
    slots = owner_slots.shape[0]
    spots = X * Y
    rows = count // spots
    spread, gain, back = tables(bins)
    spread_h, spread_l = high_low(spread)
    back_h, back_l = high_low(back)
    src_rank = lax.axis_index("core")
    ch_rank = lax.axis_index(CHIPS)
    my_plane = lax.axis_index("z")
    my_spot = lax.axis_index(PLANE)
    mine = lax.dynamic_slice_in_dim(source_ids, src_rank * count, count, 0)
    chip, plane, spot = where_of(mine, local)
    key = (plane * spots + spot) * count + lax.iota(jnp.int32, count)
    rank = jnp.sum((key[None, :] < key[:, None]).astype(jnp.int32), axis=1)
    dest = rank % spots
    flat = spectra.reshape(local, 2 * bins)

    row = lax.broadcasted_iota(jnp.int32, (spots, 1), 0)
    owned = jnp.where(chip == ch_rank, mine % local, -1)
    channel = jnp.max(jnp.where(dest[None, :] == row, owned[None, :], -1), axis=1)
    picked = select_rows(channel[:, None] == lax.broadcasted_iota(jnp.int32, (1, local), 1), flat)
    picked = by_class(picked.reshape(spots, 2, bins)).reshape(spots, 2 * bins)
    came = lax.all_to_all(picked, PLANE, 0, 0, tiled=True)

    before = jnp.sum((plane[None, :] < lax.broadcasted_iota(jnp.int32, (Z, 1), 0)).astype(jnp.int32), axis=1)
    first = before + (my_spot - before) % spots
    first_of = jnp.sum(jnp.where(plane[:, None] == lax.broadcasted_iota(jnp.int32, (1, Z), 1), first[None, :], 0), axis=1)
    turn = (rank - first_of) // spots
    here = (plane == my_plane) & (dest == my_spot)
    at = here[None, :] & (turn[None, :] == lax.broadcasted_iota(jnp.int32, (ROUNDS, 1), 0))
    sender = jnp.max(jnp.where(at, spot[None, :], -1), axis=1)
    kept = select_rows(sender[:, None] == lax.broadcasted_iota(jnp.int32, (1, spots), 1), came)
    wide = jnp.broadcast_to(kept[None], (Z,) + kept.shape)
    came = lax.all_to_all(wide, "z", 0, 0, tiled=True).reshape(Z * ROUNDS, 2 * bins)

    at = rank[None, :] == lax.broadcasted_iota(jnp.int32, (rows, 1), 0) * spots + my_spot
    sender = jnp.max(jnp.where(at, (plane * ROUNDS + turn)[None, :], -1), axis=1)
    kept = select_rows(sender[:, None] == lax.broadcasted_iota(jnp.int32, (1, Z * ROUNDS), 1), came)

    def dense():
        t = lax.iota(jnp.int32, count)
        _, z, d = where_of(t, 1)
        ids = jnp.sum(jnp.where(rank[None, :] == (z * spots + d)[:, None], mine[None, :], 0), axis=1)
        chan_ids = ch_rank * local + lax.broadcasted_iota(jnp.int32, (1, local), 1)
        found = select_rows(ids[:, None] == chan_ids, flat)
        home = jnp.sum(lax.all_to_all(found, CHIPS, 0, 0, tiled=True), axis=0, keepdims=True)
        home = by_class(home.reshape(1, 2, bins)).reshape(1, 2 * bins)
        return lax.all_to_all(jnp.broadcast_to(home, (rows, 2 * bins)), "z", 0, 0, tiled=True)

    ok = fits(source_ids[:count], local) & fits(source_ids[count:], local)
    kept = lax.cond(ok, lambda: kept, dense)
    place = dest * rows + rank // spots
    placing = place[:, None] == lax.broadcasted_iota(jnp.int32, (count, count), 1)
    iota = lax.broadcasted_iota(jnp.int32, (slots, 1), 0)
    bin_of = jnp.sum(jnp.where(iota == owner_slots[None, :], lax.broadcasted_iota(jnp.int32, (1, slots), 1), 0), axis=1)
    bins_here = select_rows(offset_bins, placing.astype(jnp.float32)).astype(jnp.int32)
    counts = bin_counts(offset_bins, slots, owner_slots)
    bin_wide = jnp.broadcast_to(bin_of[:, None], (slots, 128))
    kept, later, bins_here, counts, bin_wide = lax.optimization_barrier((kept, flat, bins_here, counts, bin_wide))
    wide = jnp.broadcast_to(kept[None], (spots,) + kept.shape)
    sources = lax.all_to_all(wide, PLANE, 0, 0, tiled=True).reshape(count, 2 * bins)
    receivers = receiver_side(later, spread_h, spread_l, jnp.asarray(gain, jnp.float32))


    panel = stacked(sources, spread_h, spread_l, receivers, bins_here, bin_wide, back_h, back_l)

    devices = X * Y * Z
    own = slots // (2 * devices)
    packed = jnp.concatenate(
        [panel.reshape(devices, 2, own * LAGS), jnp.pad(counts.reshape(devices, 2, own), ((0, 0), (0, 0), (0, LAGS - own)))],
        axis=2,
    )
    here = lax.dynamic_index_in_dim(packed, src_rank, 1, keepdims=False)
    there = lax.dynamic_index_in_dim(packed, 1 - src_rank, 1, keepdims=False)
    halves = here + lax.ppermute(there, "core", [(0, 1), (1, 0)])
    total = jnp.sum(lax.all_to_all(halves, CHIPS, 0, 0, tiled=True), axis=0)
    stack_sum = total[: own * LAGS].reshape(own, LAGS)
    stack_count = total[own * LAGS : own * LAGS + own]
    return stack_sum / jnp.sqrt(jnp.maximum(stack_count, 1.0))[:, None]


def solution(mesh):
    fine = Mesh(mesh.devices.reshape(X, Z, Y, 2), ("x", "z", "y", "core"))
    placed = (P(CHIPS, None, None), P(), P(CHIPS, "core"), P())
    return jax.shard_map(
        per_device, mesh=fine, in_specs=placed, out_specs=P(CHIPS + ("core",), None), check_vma=False
    )
```

```python
import functools

import jax
import jax.numpy as jnp
import numpy as np
from jax import lax
from jax.experimental import pallas as pl
from jax.experimental.pallas import tpu as pltpu
from jax.sharding import Mesh
from jax.sharding import PartitionSpec as P

LAGS = 128
CLASSES = 16
FFT = 256
WIDTH = 128
HALF = FFT // 2
PARTS = 4 * CLASSES
W_STEP = PARTS + 8
P_STEP = FFT + 8
X, Z, Y = 4, 8, 4
PLANE = ("x", "y")
CHIPS = ("x", "z", "y")
ROUNDS = 2
GROUPS = 4
highest = lax.Precision.HIGHEST


def tables(bins):
    q = np.arange(WIDTH)
    f = np.arange(FFT)
    low = f[:HALF]
    minus = (-low) % FFT
    spread = np.zeros((CLASSES, 4, HALF, 2, WIDTH))
    gain = np.zeros((CLASSES, 4, HALF))
    for p in range(CLASSES):
        k = CLASSES * q + p
        d = np.exp(2j * np.pi * (np.outer(k, q) % bins) / bins) @ np.exp(-2j * np.pi * (np.outer(q, f) % FFT) / FFT)
        plus, back = d[:, :HALF].T.copy(), d[:, minus].T.conj().copy()
        spread[p, 0, :, 0], spread[p, 0, :, 1] = plus.real, -plus.imag
        spread[p, 1, :, 0], spread[p, 1, :, 1] = plus.imag, plus.real
        spread[p, 2, :, 0], spread[p, 2, :, 1] = back.real, back.imag
        spread[p, 3, :, 0], spread[p, 3, :, 1] = back.imag, -back.real
        last = d[:, HALF]
        spread[p, 2, 0, 0], spread[p, 2, 0, 1] = last.real, -last.imag
        spread[p, 3, 0, 0], spread[p, 3, 0, 1] = last.imag, last.real
        odd = low % 2 == 1
        gain[p] = np.where(odd, np.sin(np.pi * p / 16), np.cos(np.pi * p / 16))
        gain[p, 2:] *= np.where(odd, -1.0, 1.0)
    j = np.arange(LAGS)
    angle = 2 * np.pi * (np.outer(low, j) % FFT) / FFT
    c, s = 2 * np.cos(angle) / FFT, 2 * np.sin(angle) / FFT
    odd = (low % 2 == 1)[:, None]
    back = np.stack([np.where(odd, s, c), np.where(odd, c, -s)])
    back[0, 0] = 2 / FFT
    back[1, 0] = 2 * np.where(j % 2 == 1, -1.0, 1.0) / FFT
    back = back.reshape(FFT, LAGS) * (CLASSES * bins ** -1.5)
    gain = gain.transpose(2, 1, 0)
    weights = np.stack([gain, gain * np.array([1.0, -1.0, 1.0, -1.0])[:, None]])
    weights[0, 0, 2:] = 0
    weights[1, 0, :2], weights[1, 0, 2:] = 0, gain[0, 2:]
    weights = np.pad(weights.reshape(2, HALF, PARTS), ((0, 0), (0, 0), (0, 128 - PARTS)))
    return spread.reshape(CLASSES, 4 * HALF, 2 * WIDTH), weights, back


def high_low(values):
    high = np.asarray(values, np.float32).astype(jnp.bfloat16)
    low = (np.asarray(values, np.float32) - high.astype(np.float32)).astype(jnp.bfloat16)
    return jnp.asarray(high), jnp.asarray(low)


def by_class(rows):
    count, two, bins = rows.shape
    return rows.reshape(count, 2, WIDTH, CLASSES).transpose(0, 3, 1, 2)


def nt(a, b):
    return lax.dot_general(a, b, (((1,), (1,)), ((), ())), preferred_element_type=jnp.float32)


def split_here(values):
    high = values.astype(jnp.bfloat16)
    return high, (values - high.astype(jnp.float32)).astype(jnp.bfloat16)


def stack_kernel(
    sources, high, low, receivers, bins_ref, slot_ref, bh_ref, bl_ref,
    out_ref, w_ref, p_ref, acc_ref, z_ref, th_ref, tl_ref, a_ref, sems,
):
    local = bins_ref.shape[0]
    group = CLASSES // GROUPS
    whole = [(sources, z_ref)]
    for g in range(GROUPS):
        part = pl.ds(g * group, group)
        whole += [(high.at[part], th_ref.at[part]), (low.at[part], tl_ref.at[part])]
    whole += [(receivers, a_ref)]
    copies = [pltpu.make_async_copy(a, b, sems.at[i]) for i, (a, b) in enumerate(whole)]
    for copy in copies:
        copy.start()
    copies[0].wait()

    for p in range(CLASSES):
        if p % group == 0:
            copies[1 + 2 * (p // group)].wait()
            copies[2 + 2 * (p // group)].wait()
        zh, zl = split_here(z_ref[:, p * 2 * WIDTH : (p + 1) * 2 * WIDTH])
        u = nt(th_ref[p], zh) + nt(tl_ref[p], zh) + nt(th_ref[p], zl)
        for c in range(4):
            w_ref[pl.ds(c * CLASSES + p, HALF, stride=W_STEP), :] = u[c * HALF : (c + 1) * HALF]

    copies[-1].wait()

    @pl.loop(0, HALF, unroll=32)
    def _(f):
        w = w_ref[pl.ds(pl.multiple_of(f * W_STEP, 8), PARTS), :].astype(jnp.bfloat16)
        o = jnp.dot(a_ref[f], jnp.concatenate([w, w], axis=0), preferred_element_type=jnp.float32)
        p_ref[pl.ds(f, local, stride=P_STEP), :] = o[:local]
        p_ref[pl.ds(f + HALF, local, stride=P_STEP), :] = o[local:]

    acc_ref[...] = jnp.zeros_like(acc_ref)
    some = 16

    @pl.loop(0, local // some)
    def _(g):
        member, prod = [], []
        for i in range(some):
            r = g * some + i
            mine = slot_ref[...] == bins_ref[pl.ds(r, 1), :]
            member.append(jnp.where(mine, 1.0, 0.0).astype(jnp.bfloat16))
            prod.append(p_ref[pl.ds(pl.multiple_of(r * P_STEP, 8), FFT), :].astype(jnp.bfloat16))
        acc_ref[...] += nt(jnp.concatenate(member, axis=1), jnp.concatenate(prod, axis=1))

    ah, al = split_here(acc_ref[...])
    out_ref[...] = (
        jnp.dot(ah, bh_ref[...], preferred_element_type=jnp.float32)
        + jnp.dot(al, bh_ref[...], preferred_element_type=jnp.float32)
        + jnp.dot(ah, bl_ref[...], preferred_element_type=jnp.float32)
    )


def stacked(sources, spread_h, spread_l, receivers, bins, bin_of, back_h, back_l):
    local = bins.shape[0]
    slots = bin_of.shape[0]
    vmem = pl.BlockSpec(memory_space=pltpu.VMEM)
    return pl.pallas_call(
        stack_kernel,
        out_shape=jax.ShapeDtypeStruct((slots, LAGS), jnp.float32),
        in_specs=[pl.BlockSpec(memory_space=pl.ANY)] * 4 + [vmem] * 4,
        out_specs=vmem,
        scratch_shapes=[
            pltpu.VMEM((HALF * W_STEP, 128), jnp.float32),
            pltpu.VMEM((local * P_STEP, 128), jnp.float32),
            pltpu.VMEM((slots, FFT), jnp.float32),
            pltpu.VMEM(sources.shape, jnp.float32),
            pltpu.VMEM(spread_h.shape, jnp.bfloat16),
            pltpu.VMEM(spread_h.shape, jnp.bfloat16),
            pltpu.VMEM(receivers.shape, jnp.bfloat16),
            pltpu.SemaphoreType.DMA((2 * GROUPS + 2,)),
        ],
        compiler_params=pltpu.CompilerParams(vmem_limit_bytes=50 * 1024 * 1024),
        cost_estimate=pl.CostEstimate(flops=9 * 10**9, bytes_accessed=16 * 2**20, transcendentals=0),
    )(sources, spread_h, spread_l, receivers, bins, bin_of, back_h, back_l)


def receiver_kernel(z_ref, th_ref, tl_ref, gain_ref, out_ref, t_ref, v_ref):
    local = z_ref.shape[0]
    block = 2 * WIDTH

    @pl.loop(0, t_ref.shape[0] // block)
    def _(i):
        at = pl.multiple_of(i * block, block)
        t_ref[pl.ds(at, block), :local] = z_ref[:, pl.ds(at, block)].T

    odd = lax.broadcasted_iota(jnp.int32, (2 * WIDTH, local), 0) % 2 == 1
    bins = t_ref.shape[0] // 2
    for p in range(CLASSES):
        z = jnp.concatenate([t_ref[pl.ds(i * bins + p, WIDTH, stride=CLASSES), :][:, :local] for i in range(2)], axis=0)
        zh, zl = split_here(jnp.where(odd, -z, z))
        u = (
            jnp.dot(th_ref[p], zh, preferred_element_type=jnp.float32)
            + jnp.dot(tl_ref[p], zh, preferred_element_type=jnp.float32)
            + jnp.dot(th_ref[p], zl, preferred_element_type=jnp.float32)
        )
        for c in range(4):
            v_ref[pl.ds(c * CLASSES + p, HALF, stride=W_STEP), :local] = u[c * HALF : (c + 1) * HALF]

    def place(f, swap):
        v = v_ref[pl.ds(pl.multiple_of(f * W_STEP, 8), PARTS), :local]
        a, b, c, d = (v[i * CLASSES : (i + 1) * CLASSES] for i in range(4))
        w = jnp.concatenate([b, a, d, c], axis=0) if swap else v
        real = v.T * gain_ref[0, pl.ds(f, 1), :PARTS]
        imag = w.T * gain_ref[1, pl.ds(f, 1), :PARTS]
        high, low = split_here(jnp.concatenate([real, imag], axis=0))
        out_ref[f] = jnp.concatenate([high, low], axis=1)

    @pl.loop(0, HALF, unroll=8)
    def _(f):
        place(f, True)

    place(0, False)


def receiver_side(flat, spread_h, spread_l, gain):
    local, width = flat.shape
    vmem = pl.BlockSpec(memory_space=pltpu.VMEM)
    return pl.pallas_call(
        receiver_kernel,
        out_shape=jax.ShapeDtypeStruct((HALF, 2 * local, 2 * PARTS), jnp.bfloat16),
        in_specs=[vmem] * 4,
        out_specs=vmem,
        scratch_shapes=[pltpu.VMEM((width, 128), jnp.float32), pltpu.VMEM((HALF * W_STEP, 128), jnp.float32)],
        compiler_params=pltpu.CompilerParams(vmem_limit_bytes=26 * 1024 * 1024),
        cost_estimate=pl.CostEstimate(flops=6 * 10**9, bytes_accessed=14 * 2**20, transcendentals=0),
    )(flat, spread_h, spread_l, gain)


def where_of(ids, local):
    chip = ids // local
    return chip, (chip // Y) % Z, (chip // (Z * Y)) * Y + chip % Y


def fits(ids, local):
    chip, plane, _ = where_of(ids, local)
    per_chip = jnp.sum((chip[:, None] == chip[None, :]).astype(jnp.int32), axis=1)
    per_plane = jnp.sum((plane[:, None] == plane[None, :]).astype(jnp.int32), axis=1)
    return (jnp.max(per_chip) <= X * Y) & (jnp.max(per_plane) <= ROUNDS * X * Y)


def select_rows(table, rows):
    return jnp.dot(table.astype(jnp.float32), rows, precision=highest, preferred_element_type=jnp.float32)


def bin_counts(bins, slots, owner_slots):
    flat = bins.reshape(1, -1)
    digit = lax.broadcasted_iota(jnp.int32, (32, 1), 0)
    high = (flat // 32 == digit).astype(jnp.bfloat16)
    low = (flat % 32 == digit).astype(jnp.bfloat16)
    per_bin = nt(high, low).reshape(1, slots)
    at = lax.broadcasted_iota(jnp.int32, (slots, 1), 0) == owner_slots[None, :]
    return jnp.sum(jnp.where(at, per_bin, 0.0), axis=1)


def per_device(spectra, source_ids, offset_bins, owner_slots):
    local, two, bins = spectra.shape
    count = offset_bins.shape[1]
    slots = owner_slots.shape[0]
    spots = X * Y
    rows = count // spots
    spread, gain, back = tables(bins)
    spread_h, spread_l = high_low(spread)
    back_h, back_l = high_low(back)
    src_rank = lax.axis_index("core")
    ch_rank = lax.axis_index(CHIPS)
    my_plane = lax.axis_index("z")
    my_spot = lax.axis_index(PLANE)
    mine = lax.dynamic_slice_in_dim(source_ids, src_rank * count, count, 0)
    chip, plane, spot = where_of(mine, local)
    key = (plane * spots + spot) * count + lax.iota(jnp.int32, count)
    rank = jnp.sum((key[None, :] < key[:, None]).astype(jnp.int32), axis=1)
    dest = rank % spots
    flat = spectra.reshape(local, 2 * bins)

    row = lax.broadcasted_iota(jnp.int32, (spots, 1), 0)
    owned = jnp.where(chip == ch_rank, mine % local, -1)
    channel = jnp.max(jnp.where(dest[None, :] == row, owned[None, :], -1), axis=1)
    picked = select_rows(channel[:, None] == lax.broadcasted_iota(jnp.int32, (1, local), 1), flat)
    picked = by_class(picked.reshape(spots, 2, bins)).reshape(spots, 2 * bins)
    came = lax.all_to_all(picked, PLANE, 0, 0, tiled=True)

    before = jnp.sum((plane[None, :] < lax.broadcasted_iota(jnp.int32, (Z, 1), 0)).astype(jnp.int32), axis=1)
    first = before + (my_spot - before) % spots
    first_of = jnp.sum(jnp.where(plane[:, None] == lax.broadcasted_iota(jnp.int32, (1, Z), 1), first[None, :], 0), axis=1)
    turn = (rank - first_of) // spots
    here = (plane == my_plane) & (dest == my_spot)
    at = here[None, :] & (turn[None, :] == lax.broadcasted_iota(jnp.int32, (ROUNDS, 1), 0))
    sender = jnp.max(jnp.where(at, spot[None, :], -1), axis=1)
    kept = select_rows(sender[:, None] == lax.broadcasted_iota(jnp.int32, (1, spots), 1), came)
    wide = jnp.broadcast_to(kept[None], (Z,) + kept.shape)
    came = lax.all_to_all(wide, "z", 0, 0, tiled=True).reshape(Z * ROUNDS, 2 * bins)

    at = rank[None, :] == lax.broadcasted_iota(jnp.int32, (rows, 1), 0) * spots + my_spot
    sender = jnp.max(jnp.where(at, (plane * ROUNDS + turn)[None, :], -1), axis=1)
    kept = select_rows(sender[:, None] == lax.broadcasted_iota(jnp.int32, (1, Z * ROUNDS), 1), came)

    def dense():
        t = lax.iota(jnp.int32, count)
        _, z, d = where_of(t, 1)
        ids = jnp.sum(jnp.where(rank[None, :] == (z * spots + d)[:, None], mine[None, :], 0), axis=1)
        chan_ids = ch_rank * local + lax.broadcasted_iota(jnp.int32, (1, local), 1)
        found = select_rows(ids[:, None] == chan_ids, flat)
        home = jnp.sum(lax.all_to_all(found, CHIPS, 0, 0, tiled=True), axis=0, keepdims=True)
        home = by_class(home.reshape(1, 2, bins)).reshape(1, 2 * bins)
        return lax.all_to_all(jnp.broadcast_to(home, (rows, 2 * bins)), "z", 0, 0, tiled=True)

    ok = fits(source_ids[:count], local) & fits(source_ids[count:], local)
    kept = lax.cond(ok, lambda: kept, dense)
    place = dest * rows + rank // spots
    placing = place[:, None] == lax.broadcasted_iota(jnp.int32, (count, count), 1)
    iota = lax.broadcasted_iota(jnp.int32, (slots, 1), 0)
    bin_of = jnp.sum(jnp.where(iota == owner_slots[None, :], lax.broadcasted_iota(jnp.int32, (1, slots), 1), 0), axis=1)
    bins_here = select_rows(offset_bins, placing.astype(jnp.float32)).astype(jnp.int32)
    counts = bin_counts(offset_bins, slots, owner_slots)
    bin_wide = jnp.broadcast_to(bin_of[:, None], (slots, 128))
    kept, later, bins_here, counts, bin_wide = lax.optimization_barrier((kept, flat, bins_here, counts, bin_wide))
    wide = jnp.broadcast_to(kept[None], (spots,) + kept.shape)
    sources = lax.all_to_all(wide, PLANE, 0, 0, tiled=True).reshape(count, 2 * bins)
    receivers = receiver_side(later, spread_h, spread_l, jnp.asarray(gain, jnp.float32))


    panel = stacked(sources, spread_h, spread_l, receivers, bins_here, bin_wide, back_h, back_l)

    devices = X * Y * Z
    own = slots // (2 * devices)
    packed = jnp.concatenate(
        [panel.reshape(devices, 2, own * LAGS), jnp.pad(counts.reshape(devices, 2, own), ((0, 0), (0, 0), (0, LAGS - own)))],
        axis=2,
    )
    here = lax.dynamic_index_in_dim(packed, src_rank, 1, keepdims=False)
    there = lax.dynamic_index_in_dim(packed, 1 - src_rank, 1, keepdims=False)
    halves = here + lax.ppermute(there, "core", [(0, 1), (1, 0)])
    total = jnp.sum(lax.all_to_all(halves, CHIPS, 0, 0, tiled=True), axis=0)
    stack_sum = total[: own * LAGS].reshape(own, LAGS)
    stack_count = total[own * LAGS : own * LAGS + own]
    return stack_sum / jnp.sqrt(jnp.maximum(stack_count, 1.0))[:, None]


def solution(mesh):
    fine = Mesh(mesh.devices.reshape(X, Z, Y, 2), ("x", "z", "y", "core"))
    placed = (P(CHIPS, None, None), P(), P(CHIPS, "core"), P())
    return jax.shard_map(
        per_device, mesh=fine, in_specs=placed, out_specs=P(CHIPS + ("core",), None), check_vma=False
    )
```

```python
import functools

import jax
import jax.numpy as jnp
import numpy as np
from jax import lax
from jax.experimental import pallas as pl
from jax.experimental.pallas import tpu as pltpu
from jax.sharding import Mesh
from jax.sharding import PartitionSpec as P

LAGS = 128
CLASSES = 16
FFT = 256
WIDTH = 128
HALF = FFT // 2
PARTS = 4 * CLASSES
W_STEP = PARTS + 8
P_STEP = FFT + 8
X, Z, Y = 4, 8, 4
PLANE = ("x", "y")
CHIPS = ("x", "z", "y")
ROUNDS = 2
GROUPS = 4
highest = lax.Precision.HIGHEST


def tables(bins):
    q = np.arange(WIDTH)
    f = np.arange(FFT)
    low = f[:HALF]
    minus = (-low) % FFT
    spread = np.zeros((CLASSES, 4, HALF, 2, WIDTH))
    gain = np.zeros((CLASSES, 4, HALF))
    for p in range(CLASSES):
        k = CLASSES * q + p
        d = np.exp(2j * np.pi * (np.outer(k, q) % bins) / bins) @ np.exp(-2j * np.pi * (np.outer(q, f) % FFT) / FFT)
        plus, back = d[:, :HALF].T.copy(), d[:, minus].T.conj().copy()
        spread[p, 0, :, 0], spread[p, 0, :, 1] = plus.real, -plus.imag
        spread[p, 1, :, 0], spread[p, 1, :, 1] = plus.imag, plus.real
        spread[p, 2, :, 0], spread[p, 2, :, 1] = back.real, back.imag
        spread[p, 3, :, 0], spread[p, 3, :, 1] = back.imag, -back.real
        last = d[:, HALF]
        spread[p, 2, 0, 0], spread[p, 2, 0, 1] = last.real, -last.imag
        spread[p, 3, 0, 0], spread[p, 3, 0, 1] = last.imag, last.real
        odd = low % 2 == 1
        gain[p] = np.where(odd, np.sin(np.pi * p / 16), np.cos(np.pi * p / 16))
        gain[p, 2:] *= np.where(odd, -1.0, 1.0)
    j = np.arange(LAGS)
    angle = 2 * np.pi * (np.outer(low, j) % FFT) / FFT
    c, s = 2 * np.cos(angle) / FFT, 2 * np.sin(angle) / FFT
    odd = (low % 2 == 1)[:, None]
    back = np.stack([np.where(odd, s, c), np.where(odd, c, -s)])
    back[0, 0] = 2 / FFT
    back[1, 0] = 2 * np.where(j % 2 == 1, -1.0, 1.0) / FFT
    back = back.reshape(FFT, LAGS) * (CLASSES * bins ** -1.5)
    gain = gain.transpose(2, 1, 0)
    weights = np.stack([gain, gain * np.array([1.0, -1.0, 1.0, -1.0])[:, None]])
    weights[0, 0, 2:] = 0
    weights[1, 0, :2], weights[1, 0, 2:] = 0, gain[0, 2:]
    weights = np.pad(weights.reshape(2, HALF, PARTS), ((0, 0), (0, 0), (0, 128 - PARTS)))
    return spread.reshape(CLASSES, 4 * HALF, 2 * WIDTH), weights, back


def high_low(values):
    high = np.asarray(values, np.float32).astype(jnp.bfloat16)
    low = (np.asarray(values, np.float32) - high.astype(np.float32)).astype(jnp.bfloat16)
    return jnp.asarray(high), jnp.asarray(low)


def by_class(rows):
    count, two, bins = rows.shape
    return rows.reshape(count, 2, WIDTH, CLASSES).transpose(0, 3, 1, 2)


def nt(a, b):
    return lax.dot_general(a, b, (((1,), (1,)), ((), ())), preferred_element_type=jnp.float32)


def split_here(values):
    high = values.astype(jnp.bfloat16)
    return high, (values - high.astype(jnp.float32)).astype(jnp.bfloat16)


def stack_kernel(
    sources, high, low, receivers, bins_ref, slot_ref, bh_ref, bl_ref,
    out_ref, w_ref, p_ref, acc_ref, z_ref, th_ref, tl_ref, a_ref, sems,
):
    local = bins_ref.shape[0]
    group = CLASSES // GROUPS
    whole = [(sources, z_ref)]
    for g in range(GROUPS):
        part = pl.ds(g * group, group)
        whole += [(high.at[part], th_ref.at[part]), (low.at[part], tl_ref.at[part])]
    whole += [(receivers, a_ref)]
    copies = [pltpu.make_async_copy(a, b, sems.at[i]) for i, (a, b) in enumerate(whole)]
    for copy in copies:
        copy.start()
    copies[0].wait()

    for p in range(CLASSES):
        if p % group == 0:
            copies[1 + 2 * (p // group)].wait()
            copies[2 + 2 * (p // group)].wait()
        zh, zl = split_here(z_ref[:, p * 2 * WIDTH : (p + 1) * 2 * WIDTH])
        u = nt(th_ref[p], zh) + nt(tl_ref[p], zh) + nt(th_ref[p], zl)
        for c in range(4):
            w_ref[pl.ds(c * CLASSES + p, HALF, stride=W_STEP), :] = u[c * HALF : (c + 1) * HALF]

    copies[-1].wait()

    @pl.loop(0, HALF, unroll=32)
    def _(f):
        w = w_ref[pl.ds(pl.multiple_of(f * W_STEP, 8), PARTS), :].astype(jnp.bfloat16)
        o = jnp.dot(a_ref[f], jnp.concatenate([w, w], axis=0), preferred_element_type=jnp.float32)
        p_ref[pl.ds(f, local, stride=P_STEP), :] = o[:local]
        p_ref[pl.ds(f + HALF, local, stride=P_STEP), :] = o[local:]

    acc_ref[...] = jnp.zeros_like(acc_ref)
    some = 16

    @pl.loop(0, local // some)
    def _(g):
        member, prod = [], []
        for i in range(some):
            r = g * some + i
            mine = slot_ref[...] == bins_ref[pl.ds(r, 1), :]
            member.append(jnp.where(mine, 1.0, 0.0).astype(jnp.bfloat16))
            prod.append(p_ref[pl.ds(pl.multiple_of(r * P_STEP, 8), FFT), :].astype(jnp.bfloat16))
        acc_ref[...] += nt(jnp.concatenate(member, axis=1), jnp.concatenate(prod, axis=1))

    ah, al = split_here(acc_ref[...])
    out_ref[...] = (
        jnp.dot(ah, bh_ref[...], preferred_element_type=jnp.float32)
        + jnp.dot(al, bh_ref[...], preferred_element_type=jnp.float32)
        + jnp.dot(ah, bl_ref[...], preferred_element_type=jnp.float32)
    )


def stacked(sources, spread_h, spread_l, receivers, bins, bin_of, back_h, back_l):
    local = bins.shape[0]
    slots = bin_of.shape[0]
    vmem = pl.BlockSpec(memory_space=pltpu.VMEM)
    return pl.pallas_call(
        stack_kernel,
        out_shape=jax.ShapeDtypeStruct((slots, LAGS), jnp.float32),
        in_specs=[pl.BlockSpec(memory_space=pl.ANY)] * 4 + [vmem] * 4,
        out_specs=vmem,
        scratch_shapes=[
            pltpu.VMEM((HALF * W_STEP, 128), jnp.float32),
            pltpu.VMEM((local * P_STEP, 128), jnp.float32),
            pltpu.VMEM((slots, FFT), jnp.float32),
            pltpu.VMEM(sources.shape, jnp.float32),
            pltpu.VMEM(spread_h.shape, jnp.bfloat16),
            pltpu.VMEM(spread_h.shape, jnp.bfloat16),
            pltpu.VMEM(receivers.shape, jnp.bfloat16),
            pltpu.SemaphoreType.DMA((2 * GROUPS + 2,)),
        ],
        compiler_params=pltpu.CompilerParams(vmem_limit_bytes=50 * 1024 * 1024),
        cost_estimate=pl.CostEstimate(flops=9 * 10**9, bytes_accessed=16 * 2**20, transcendentals=0),
    )(sources, spread_h, spread_l, receivers, bins, bin_of, back_h, back_l)


def receiver_kernel(z_ref, th_ref, tl_ref, gain_ref, out_ref, t_ref, v_ref):
    local = z_ref.shape[0]
    block = 2 * WIDTH

    @pl.loop(0, t_ref.shape[0] // block)
    def _(i):
        at = pl.multiple_of(i * block, block)
        t_ref[pl.ds(at, block), :local] = z_ref[:, pl.ds(at, block)].T

    odd = lax.broadcasted_iota(jnp.int32, (2 * WIDTH, local), 0) % 2 == 1
    bins = t_ref.shape[0] // 2
    for p in range(CLASSES):
        z = jnp.concatenate([t_ref[pl.ds(i * bins + p, WIDTH, stride=CLASSES), :][:, :local] for i in range(2)], axis=0)
        zh, zl = split_here(jnp.where(odd, -z, z))
        u = (
            jnp.dot(th_ref[p], zh, preferred_element_type=jnp.float32)
            + jnp.dot(tl_ref[p], zh, preferred_element_type=jnp.float32)
            + jnp.dot(th_ref[p], zl, preferred_element_type=jnp.float32)
        )
        for c in range(4):
            v_ref[pl.ds(c * CLASSES + p, HALF, stride=W_STEP), :local] = u[c * HALF : (c + 1) * HALF]

    def place(f, swap):
        v = v_ref[pl.ds(pl.multiple_of(f * W_STEP, 8), PARTS), :local]
        a, b, c, d = (v[i * CLASSES : (i + 1) * CLASSES] for i in range(4))
        w = jnp.concatenate([b, a, d, c], axis=0) if swap else v
        real = v.T * gain_ref[0, pl.ds(f, 1), :PARTS]
        imag = w.T * gain_ref[1, pl.ds(f, 1), :PARTS]
        high, low = split_here(jnp.concatenate([real, imag], axis=0))
        out_ref[f] = jnp.concatenate([high, low], axis=1)

    @pl.loop(0, HALF, unroll=8)
    def _(f):
        place(f, True)

    place(0, False)


def receiver_side(flat, spread_h, spread_l, gain):
    local, width = flat.shape
    vmem = pl.BlockSpec(memory_space=pltpu.VMEM)
    return pl.pallas_call(
        receiver_kernel,
        out_shape=jax.ShapeDtypeStruct((HALF, 2 * local, 2 * PARTS), jnp.bfloat16),
        in_specs=[vmem] * 4,
        out_specs=vmem,
        scratch_shapes=[pltpu.VMEM((width, 128), jnp.float32), pltpu.VMEM((HALF * W_STEP, 128), jnp.float32)],
        compiler_params=pltpu.CompilerParams(vmem_limit_bytes=26 * 1024 * 1024),
        cost_estimate=pl.CostEstimate(flops=6 * 10**9, bytes_accessed=14 * 2**20, transcendentals=0),
    )(flat, spread_h, spread_l, gain)


def where_of(ids, local):
    chip = ids // local
    return chip, (chip // Y) % Z, (chip // (Z * Y)) * Y + chip % Y


def fits(ids, local):
    chip, plane, _ = where_of(ids, local)
    per_chip = jnp.sum((chip[:, None] == chip[None, :]).astype(jnp.int32), axis=1)
    per_plane = jnp.sum((plane[:, None] == plane[None, :]).astype(jnp.int32), axis=1)
    return (jnp.max(per_chip) <= X * Y) & (jnp.max(per_plane) <= ROUNDS * X * Y)


def select_rows(table, rows):
    return jnp.dot(table.astype(jnp.float32), rows, precision=highest, preferred_element_type=jnp.float32)


def bin_counts(bins, slots, owner_slots, slot_of):
    flat = bins.reshape(1, -1)
    digit = lax.broadcasted_iota(jnp.int32, (32, 1), 0)
    high = (flat // 32 == digit).astype(jnp.bfloat16)
    low = (flat % 32 == digit).astype(jnp.bfloat16)
    per_bin = nt(high, low).reshape(1, slots)
    at = slot_of == owner_slots[None, :]
    return jnp.sum(jnp.where(at, per_bin, 0.0), axis=1)


def per_device(spectra, source_ids, offset_bins, owner_slots):
    local, two, bins = spectra.shape
    count = offset_bins.shape[1]
    slots = owner_slots.shape[0]
    spots = X * Y
    rows = count // spots
    spread, gain, back = tables(bins)
    spread_h, spread_l = high_low(spread)
    back_h, back_l = high_low(back)
    src_rank = lax.axis_index("core")
    ch_rank = lax.axis_index(CHIPS)
    my_plane = lax.axis_index("z")
    my_spot = lax.axis_index(PLANE)
    mine = lax.dynamic_slice_in_dim(source_ids, src_rank * count, count, 0)
    chip, plane, spot = where_of(mine, local)
    key = (plane * spots + spot) * count + lax.iota(jnp.int32, count)
    rank = jnp.sum((key[None, :] < key[:, None]).astype(jnp.int32), axis=1)
    dest = rank % spots
    flat = spectra.reshape(local, 2 * bins)

    row = lax.broadcasted_iota(jnp.int32, (spots, 1), 0)
    owned = jnp.where(chip == ch_rank, mine % local, -1)
    channel = jnp.max(jnp.where(dest[None, :] == row, owned[None, :], -1), axis=1)
    picked = select_rows(channel[:, None] == lax.broadcasted_iota(jnp.int32, (1, local), 1), flat)
    picked = by_class(picked.reshape(spots, 2, bins)).reshape(spots, 2 * bins)
    came = lax.all_to_all(picked, PLANE, 0, 0, tiled=True)

    before = jnp.sum((plane[None, :] < lax.broadcasted_iota(jnp.int32, (Z, 1), 0)).astype(jnp.int32), axis=1)
    first = before + (my_spot - before) % spots
    first_of = jnp.sum(jnp.where(plane[:, None] == lax.broadcasted_iota(jnp.int32, (1, Z), 1), first[None, :], 0), axis=1)
    turn = (rank - first_of) // spots
    here = (plane == my_plane) & (dest == my_spot)
    at = here[None, :] & (turn[None, :] == lax.broadcasted_iota(jnp.int32, (ROUNDS, 1), 0))
    sender = jnp.max(jnp.where(at, spot[None, :], -1), axis=1)
    kept = select_rows(sender[:, None] == lax.broadcasted_iota(jnp.int32, (1, spots), 1), came)
    wide = jnp.broadcast_to(kept[None], (Z,) + kept.shape)
    came = lax.all_to_all(wide, "z", 0, 0, tiled=True).reshape(Z * ROUNDS, 2 * bins)

    at = rank[None, :] == lax.broadcasted_iota(jnp.int32, (rows, 1), 0) * spots + my_spot
    sender = jnp.max(jnp.where(at, (plane * ROUNDS + turn)[None, :], -1), axis=1)
    kept = select_rows(sender[:, None] == lax.broadcasted_iota(jnp.int32, (1, Z * ROUNDS), 1), came)

    def dense():
        t = lax.iota(jnp.int32, count)
        _, z, d = where_of(t, 1)
        ids = jnp.sum(jnp.where(rank[None, :] == (z * spots + d)[:, None], mine[None, :], 0), axis=1)
        chan_ids = ch_rank * local + lax.broadcasted_iota(jnp.int32, (1, local), 1)
        found = select_rows(ids[:, None] == chan_ids, flat)
        home = jnp.sum(lax.all_to_all(found, CHIPS, 0, 0, tiled=True), axis=0, keepdims=True)
        home = by_class(home.reshape(1, 2, bins)).reshape(1, 2 * bins)
        return lax.all_to_all(jnp.broadcast_to(home, (rows, 2 * bins)), "z", 0, 0, tiled=True)

    ok = fits(source_ids[:count], local) & fits(source_ids[count:], local)
    kept = lax.cond(ok, lambda: kept, dense)
    place = dest * rows + rank // spots
    placing = place[:, None] == lax.broadcasted_iota(jnp.int32, (count, count), 1)
    devices = X * Y * Z
    own = slots // (2 * devices)
    line = lax.broadcasted_iota(jnp.int32, (slots, 1), 0)
    block = devices * own
    slot_of = (line % block // own * 2 + (line // block + src_rank) % 2) * own + line % own
    bin_of = jnp.sum(jnp.where(slot_of == owner_slots[None, :], lax.broadcasted_iota(jnp.int32, (1, slots), 1), 0), axis=1)
    bins_here = select_rows(offset_bins, placing.astype(jnp.float32)).astype(jnp.int32)
    counts = bin_counts(offset_bins, slots, owner_slots, slot_of)
    bin_wide = jnp.broadcast_to(bin_of[:, None], (slots, 128))
    kept, later, bins_here, counts, bin_wide = lax.optimization_barrier((kept, flat, bins_here, counts, bin_wide))
    wide = jnp.broadcast_to(kept[None], (spots,) + kept.shape)
    sources = lax.all_to_all(wide, PLANE, 0, 0, tiled=True).reshape(count, 2 * bins)
    receivers = receiver_side(later, spread_h, spread_l, jnp.asarray(gain, jnp.float32))


    panel = stacked(sources, spread_h, spread_l, receivers, bins_here, bin_wide, back_h, back_l)

    counted = jnp.pad(counts.reshape(2, devices, own), ((0, 0), (0, 0), (0, LAGS - own)))
    here, there = (
        jnp.concatenate([panel[i * block : (i + 1) * block].reshape(devices, own * LAGS), counted[i]], axis=1)
        for i in range(2)
    )
    both = here + lax.ppermute(there, "core", [(0, 1), (1, 0)])
    total = jnp.sum(lax.all_to_all(both, CHIPS, 0, 0, tiled=True), axis=0)
    stack_sum = total[: own * LAGS].reshape(own, LAGS)
    stack_count = total[own * LAGS : own * LAGS + own]
    return stack_sum / jnp.sqrt(jnp.maximum(stack_count, 1.0))[:, None]


def solution(mesh):
    fine = Mesh(mesh.devices.reshape(X, Z, Y, 2), ("x", "z", "y", "core"))
    placed = (P(CHIPS, None, None), P(), P(CHIPS, "core"), P())
    return jax.shard_map(
        per_device, mesh=fine, in_specs=placed, out_specs=P(CHIPS + ("core",), None), check_vma=False
    )
```
